512 devices in a mesh: fsdp: 8 (over y_lo, x), seq: 64 (over z, y_hi, core).
Axes of the slice: x: 4, y: 8 (y_hi: 4, y_lo: 2; y = y_hi * 2 + y_lo), z: 8, core: 2. Of those that a mesh axis runs over, the one named last changes fastest.
Arguments:
- q_heads: bfloat16 [8192, 5120], P('seq', 'fsdp'), may hold values from -5 to 5
- k_heads: bfloat16 [8192, 5120], P('seq', 'fsdp'), may hold values from -5 to 5
- v_heads: bfloat16 [8192, 5120], P('seq', 'fsdp'), may hold values from -16 to 16
- out_weight: bfloat16 [5120, 5120], P('fsdp', 'seq'), may hold values from -0.078125 to 0.078125
- out_gate: float32 [5120], P('fsdp'), may hold values from 2 to 20
- tile_map: int32 [64], replicated, may hold values from 0 to 63, as said below
- key_tiles: int32 [64, 4], replicated, may hold values from 0 to 63, as said below
- key_count: int32 [64], replicated, may hold values from 1 to 4, as said below
Outputs:
- attn_out: bfloat16 [5120, 8192], P('fsdp', 'seq')
The draws below stay inside these ranges and needn't reach their ends.
Inputs may be any that keep to these rules, and one draw needn't show every extreme that they name: `tile_map`: slots 2 * p to 2 * (p + 1) - 1 hold the tiles 2 * p to 2 * (p + 1) - 1 in some order; every tile is held once. `key_tiles`: row t starts with t itself; its entries are distinct tiles u with |u // 2 - t // 2| <= 1; only the first key_count[t] entries are used. `key_count`: some tile uses all 4 entries.
All inputs are finite; a program needn't handle non-finite values.
Results may differ from the reference program's by a relative error of at most 0.02.
Values may be sent and summed in bfloat16 or wider, within the bound.
A program may use at most 64 MiB of HBM per device.

```python
import math
import jax
import jax.numpy as jnp
from jax import lax

D = 5120
HEADS = 40
HD = 128
TILE = 128
GT = 32
TILES = 64
TOKENS = 8192
PLANE = 2
KMAX = 4
N_FSDP = 8


def drawn_values(key):
    return jnp.clip(jax.random.normal(jax.random.fold_in(key, 3), (TOKENS, HEADS * HD), jnp.float32), -5.0, 5.0)


def draw_q_heads(key, part):
    drawn = drawn_values(jax.random.fold_in(key, 41))
    return drawn.astype(jnp.bfloat16)


def draw_k_heads(key, part):
    drawn = drawn_values(jax.random.fold_in(key, 43))
    return drawn.astype(jnp.bfloat16)


def draw_tile_map(key, part):
    scores = jax.random.randint(jax.random.fold_in(key, 51), (GT, PLANE), 0, 1 << 20)
    keyed = scores * PLANE + jnp.arange(PLANE, dtype=jnp.int32)[None, :]
    order_rows = jnp.argsort(keyed, axis=1)
    placed = order_rows + jnp.arange(GT, dtype=jnp.int32)[:, None] * PLANE
    return placed.reshape(TILES).astype(jnp.int32)


def draw_key_tiles(key, part):
    tile_index = jnp.arange(TILES, dtype=jnp.int32)
    plane_index = tile_index // PLANE
    near_plane = jnp.abs(plane_index[:, None] - plane_index[None, :]) <= 1
    candidate = near_plane & (tile_index[:, None] != tile_index[None, :])
    scores = jax.random.randint(jax.random.fold_in(key, 61), (TILES, TILES), 0, 1 << 20) * TILES + tile_index[None, :]
    scores = jnp.where(candidate, scores, -1 - tile_index[None, :])
    picked = lax.top_k(scores, KMAX - 1)[1].astype(jnp.int32)
    return jnp.concatenate([tile_index[:, None], picked], axis=1).astype(jnp.int32)


def draw_key_count(key, part):
    lengths = jax.random.randint(jax.random.fold_in(key, 71), (TILES,), 1, KMAX + 1)
    fullest = jax.random.randint(jax.random.fold_in(key, 73), (), 0, TILES)
    return lengths.at[fullest].set(KMAX).astype(jnp.int32)


def levels(key, shape, split, low, top_value):
    loudness, own = 1.0, jax.random.fold_in(key, 6)
    for axis_at, blocks in split:
        heights = jnp.exp(jax.random.uniform(jax.random.fold_in(own, axis_at), (blocks,), jnp.float32, low / len(split), top_value / len(split)))
        loudness = loudness * jnp.repeat(heights, shape[axis_at] // blocks).reshape([-1 if axis == axis_at else 1 for axis in range(len(shape))])
    return loudness


def noise(rng, extent, spread, limit, split=(), kind=jnp.bfloat16):
    entries = spread * jax.random.normal(rng, extent, jnp.float32)
    if split:
        entries = entries * levels(rng, extent, split, -0.22, 0.18)
    return jnp.clip(entries, -limit, limit).astype(kind)


def setup_inputs(seed: int = 0) -> dict:
    splits = jax.random.split(jax.random.key(seed), 9)
    q_heads = draw_q_heads(jax.random.fold_in(splits[8], 71), 0)
    k_heads = draw_k_heads(jax.random.fold_in(splits[8], 71), 0)
    v_heads = noise(splits[2], (TOKENS, HEADS * HD), 4.0, 16.0, ((0, 64), (1, 8)))
    out_weight = noise(splits[3], (HEADS * HD, D), (HEADS * HD) ** -0.5, 0.078125, ((0, 8), (1, 64)))
    out_gate = jnp.clip(jnp.exp(math.log(20.0) - 2.3025851 * jax.random.uniform(splits[4], (D,), jnp.float32) ** levels(splits[4], (D,), ((0, 8),), -0.2, 0.2)), 2.0, 20.0)
    tile_map = draw_tile_map(jax.random.fold_in(splits[8], 71), 0)
    key_tiles = draw_key_tiles(jax.random.fold_in(splits[8], 71), 0)
    key_count = draw_key_count(jax.random.fold_in(splits[8], 71), 0)
    return {"q_heads": q_heads, "k_heads": k_heads, "v_heads": v_heads, "out_weight": out_weight, "out_gate": out_gate, "tile_map": tile_map, "key_tiles": key_tiles, "key_count": key_count}


neg_large = -1e+30

def reference(q_heads, k_heads, v_heads, out_weight, out_gate, tile_map, key_tiles, key_count):
    slot_of = jnp.zeros((TILES,), jnp.int32).at[tile_map].set(jnp.arange(TILES, dtype=jnp.int32))
    query_all = q_heads.reshape(TILES, TILE, HEADS, HD)
    key_all = k_heads.reshape(TILES, TILE, HEADS * HD)
    value_all = v_heads.reshape(TILES, TILE, HEADS * HD)

    def one_tile(slot_id):
        tile_id = tile_map[slot_id]
        listed = key_tiles[tile_id]
        list_length = key_count[tile_id]
        key_slots = slot_of[listed].astype(jnp.int32)
        near_keys = key_all[key_slots].reshape(KMAX * TILE, HEADS, HD).astype(jnp.float32)
        near_values = value_all[key_slots].reshape(KMAX * TILE, HEADS, HD).astype(jnp.float32)
        valid_keys = jnp.repeat(jnp.arange(KMAX, dtype=jnp.int32) < list_length, TILE)
        scores = jnp.einsum('qhd,khd->hqk', query_all[slot_id].astype(jnp.float32), near_keys) / jnp.sqrt(jnp.float32(HD))
        masked = jnp.where(valid_keys[None, None, :], scores, neg_large)
        row_max = lax.optimization_barrier(jnp.max(masked, axis=2, keepdims=True))
        exponent = jnp.where(valid_keys[None, None, :], jnp.exp(masked - row_max), 0.0)
        totals = lax.optimization_barrier(jnp.sum(exponent, axis=2))
        weights = lax.optimization_barrier(exponent.astype(jnp.bfloat16)).astype(jnp.float32)
        mixed = jnp.einsum('hqk,khd->qhd', weights, near_values) / jnp.transpose(totals)[:, :, None]
        return mixed.reshape(TILE, HEADS * HD).astype(jnp.bfloat16)
    attention = lax.map(one_tile, jnp.arange(TILES, dtype=jnp.int32)).reshape(TOKENS, HEADS * HD)
    group_width = HEADS * HD // N_FSDP
    summed = jnp.zeros((TOKENS, D), jnp.float32)
    for group_index in range(N_FSDP):
        partial_value = jnp.dot(attention[:, group_index * group_width:(group_index + 1) * group_width], out_weight[group_index * group_width:(group_index + 1) * group_width], preferred_element_type=jnp.float32)
        summed = summed + lax.optimization_barrier(partial_value.astype(jnp.bfloat16)).astype(jnp.float32)
    return (out_gate[:, None] * jnp.transpose(summed)).astype(jnp.bfloat16)
```

```python
import functools
import jax
import jax.numpy as jnp
from jax import lax
from jax.experimental import pallas as pl
from jax.experimental.pallas import tpu as pltpu
from jax.sharding import PartitionSpec as P

HD = 128
TILE = 128
KMAX = 4
NX, NYL, NZ, NYH = 4, 2, 8, 4
PLANES = NZ * NYH
NEG = -1e30
HALVES = ((0, 48), (48, 32))
MESH = pl.DeviceIdType.MESH


def plus_hops(piece, half):
    return 4 if (piece + half) % 2 == 0 else 3


def kernel(
    q_ref, k_ref, v_ref, w_ref, gate_ref, map_ref, list_ref, count_ref, out_ref,
    kbuf, vbuf, wall, attn, obuf, xbuf, sbuf, fbuf, gcol, send_sems, recv_sems,
):
    heads = q_ref.shape[1] // HD
    wcols = w_ref.shape[0]
    f = lax.axis_index("fsdp")
    s = lax.axis_index("seq")
    yl, x = f // NX, f % NX
    core, yh, z = s % 2, (s // 2) % NYH, s // 8
    plane = s // 2

    def seq_id(zz, yy, cc):
        return zz * 8 + yy * 2 + cc

    def wrap(a, n):
        return (a + n) % n

    sibling = (f, seq_id(z, yh, 1 - core))
    z_next = (f, seq_id(wrap(z + 1, NZ), yh, core))
    z_prev = (f, seq_id(wrap(z - 1, NZ), yh, core))
    y_next = (f, seq_id(z, wrap(yh + 1, NYH), core))
    y_prev = (f, seq_id(z, wrap(yh - 1, NYH), core))
    p_next = (f, wrap(plane + 1, PLANES) * 2 + core)
    p_prev = (f, wrap(plane - 1, PLANES) * 2 + core)
    x_peer = [(yl * NX + wrap(x + r, NX), s) for r in range(NX)]
    y_same = ((1 - yl) * NX + x, s)
    y_cross = ((1 - yl) * NX + x, seq_id(z, yh, 1 - core))

    peers = [sibling, z_next, z_prev, y_next, y_prev, p_next, p_prev,
             x_peer[1], x_peer[2], x_peer[3], y_same, y_cross]
    barrier = pltpu.get_barrier_semaphore()
    for peer in peers:
        pl.semaphore_signal(barrier, inc=1, device_id=peer, device_id_type=MESH)

    kbuf[0] = k_ref[...]
    vbuf[0] = v_ref[...]
    wall[0, z] = w_ref[...]
    rows = lax.broadcasted_iota(jnp.int32, (HD, HD), 0)
    cols = lax.broadcasted_iota(jnp.int32, (HD, HD), 1)
    for i in range(gate_ref.shape[1] // HD):
        line = jnp.broadcast_to(gate_ref[:, i * HD:(i + 1) * HD], (HD, HD))
        column = jnp.sum(jnp.where(rows == cols, line, 0.0), axis=1, keepdims=True)
        gcol[i * HD:(i + 1) * HD, :] = jnp.broadcast_to(column, (HD, HD))

    pl.semaphore_wait(barrier, len(peers))

    started = []
    table = {}

    def number(key):
        return table.setdefault(key, len(table))

    def send(key, src, dst, peer):
        n = number(key)
        copy = pltpu.make_async_remote_copy(
            src_ref=src, dst_ref=dst, send_sem=send_sems.at[n], recv_sem=recv_sems.at[n],
            device_id=peer, device_id_type=MESH,
        )
        copy.start()
        started.append(copy)

    def receive(key, dst):
        n = number(key)
        pltpu.make_async_remote_copy(
            src_ref=dst, dst_ref=dst, send_sem=send_sems.at[n], recv_sem=recv_sems.at[n],
            device_id=sibling, device_id_type=MESH,
        ).wait_recv()

    def part(piece, zz, half):
        start, size = HALVES[half]
        return wall.at[piece, zz, pl.ds(start, size)]

    def ring_pieces(hop):
        return ((0, wrap(z - hop, NZ)), (1, wrap(z + hop, NZ)))

    def hops(piece, half, way):
        n = plus_hops(piece, half)
        return n if way == 0 else NZ - 1 - n

    def ring_receive(piece, hop):
        for half in range(2):
            for way, zz in ring_pieces(hop):
                if hop <= hops(piece, half, way):
                    receive(("z", piece, half, way, hop), part(piece, zz, half))

    def ring_step(piece, hop):
        for half in range(2):
            for way, zz in ring_pieces(hop - 1):
                last = hops(piece, half, way)
                if hop > 1 and hop - 1 <= last:
                    receive(("z", piece, half, way, hop - 1), part(piece, zz, half))
                if hop <= last:
                    ref = part(piece, zz, half)
                    send(("z", piece, half, way, hop), ref, ref, (z_next, z_prev)[way])

    def ring_last(piece):
        for half in range(2):
            for way in range(2):
                if hops(piece, half, way) == 4:
                    zz = ring_pieces(4)[way][1]
                    receive(("z", piece, half, way, 4), part(piece, zz, half))

    send(("y", 1), w_ref, wall.at[1, z], y_next)
    send(("y", 2), w_ref, wall.at[2, z], y_prev)
    ring_step(0, 1)
    send("ksib", k_ref, kbuf.at[1], sibling)
    send("vsib", v_ref, vbuf.at[1], sibling)
    send("kup", k_ref, kbuf.at[2], p_next)
    send("kdown", k_ref, kbuf.at[4], p_prev)
    send("vup", v_ref, vbuf.at[2], p_next)
    send("vdown", v_ref, vbuf.at[4], p_prev)

    def forward(name, buf):
        receive(name + "up", buf.at[2])
        send(name + "upfwd", buf.at[2], buf.at[3], sibling)
        receive(name + "down", buf.at[4])
        send(name + "downfwd", buf.at[4], buf.at[5], sibling)

    def attention_wait():
        for name, buf in (("k", kbuf), ("v", vbuf)):
            receive(name + "sib", buf.at[1])
            receive(name + "upfwd", buf.at[3])
            receive(name + "downfwd", buf.at[5])

    def key_bias():
        tile = map_ref[s]
        used = count_ref[tile]
        listed = [list_ref[tile, i] for i in range(KMAX)]
        below, above = wrap(plane - 1, PLANES), wrap(plane + 1, PLANES)
        slots = (
            (s, None), (plane * 2 + 1 - core, None),
            (below * 2 + core, plane > 0), (below * 2 + 1 - core, plane > 0),
            (above * 2 + core, plane < PLANES - 1), (above * 2 + 1 - core, plane < PLANES - 1),
        )
        lane_tile = lax.broadcasted_iota(jnp.int32, (1, 6 * TILE), 1) // TILE
        bias = jnp.zeros((1, 6 * TILE), jnp.float32)
        for n, (slot, inside) in enumerate(slots):
            other = map_ref[slot]
            hit = jnp.int32(0)
            for i in range(KMAX):
                same = jnp.where(listed[i] == other, 1, 0) * jnp.where(used > i, 1, 0)
                hit = jnp.maximum(hit, same)
            if inside is not None:
                hit = hit * jnp.where(inside, 1, 0)
            value = jnp.where(hit == 1, 0.0, NEG).astype(jnp.float32)
            bias = jnp.where(lane_tile == n, value, bias)
        return bias

    def attention_head(h, bias):
        span = slice(h * HD, (h + 1) * HD)
        keys = kbuf[:, :, span].reshape(6 * TILE, HD)
        values = vbuf[:, :, span].reshape(6 * TILE, HD)
        scores = lax.dot_general(
            q_ref[:, span], keys, (((1,), (1,)), ((), ())), preferred_element_type=jnp.float32
        )
        scores = scores * (1.0 / float(HD) ** 0.5) + bias
        top = jnp.max(scores, axis=1, keepdims=True)
        expo = jnp.exp(scores - top)
        total = jnp.sum(expo, axis=1, keepdims=True)
        mixed = jnp.dot(expo.astype(jnp.bfloat16), values, preferred_element_type=jnp.float32)
        attn[core, :, span] = (mixed / total).astype(jnp.bfloat16)

    def project(piece):
        weights = wall[piece].reshape(NZ * wcols, heads * HD)
        tokens = attn[...].reshape(2 * TILE, heads * HD)
        partial = lax.dot_general(
            weights, tokens, (((1,), (1,)), ((), ())), preferred_element_type=jnp.float32
        ).astype(jnp.bfloat16)
        for b in range(NZ):
            obuf[piece, b % NX, b // NX] = partial[b * wcols:(b + 1) * wcols]
        for r in (2, 1, 3):
            send(("x", piece, r), obuf.at[piece, wrap(x + r, NX)], xbuf.at[piece, r - 1], x_peer[r])

    def reduce_x(piece):
        total = obuf[piece, x].astype(jnp.float32)
        for r in (1, 3, 2):
            receive(("x", piece, r), xbuf.at[piece, r - 1])
            total = total + xbuf[piece, r - 1].astype(jnp.float32)
        total = total.astype(jnp.bfloat16)
        for t in range(2):
            sbuf[piece, :, t] = total[:, :, t * TILE:(t + 1) * TILE]
        send(("f", piece, 1), sbuf.at[piece, 1 - yl, core], fbuf.at[piece, 1], y_same)
        send(("f", piece, 2), sbuf.at[piece, 1 - yl, 1 - core], fbuf.at[piece, 2], y_cross)
        send(("f", piece, 3), sbuf.at[piece, yl, 1 - core], fbuf.at[piece, 0], sibling)

    def finish(piece):
        receive(("f", piece, 1), fbuf.at[piece, 1])
        receive(("f", piece, 2), fbuf.at[piece, 2])
        receive(("f", piece, 3), fbuf.at[piece, 0])
        from_yh = wrap(yh + (0, -1, 1, 2)[piece], NYH)
        for other in range(2):
            c = core if other == 0 else 1 - core
            start = pl.multiple_of(from_yh * (2 * wcols) + c * wcols, 16)
            near = sbuf[piece, yl, core] if other == 0 else fbuf[piece, 0]
            far = fbuf[piece, 1] if other == 0 else fbuf[piece, 2]
            summed = near.astype(jnp.float32) + far.astype(jnp.float32)
            gate = gcol[pl.ds(start, wcols), :]
            out_ref[pl.ds(start, wcols), :] = (gate * summed).astype(out_ref.dtype)

    ring_step(0, 2)
    ring_step(0, 3)
    receive(("y", 1), wall.at[1, z])
    ring_step(1, 1)
    start, size = HALVES[0]
    send(("y", 3), wall.at[1, z, pl.ds(start, size)], wall.at[3, z, pl.ds(start, size)], y_next)
    ring_step(0, 4)
    receive(("y", 2), wall.at[2, z])
    start, size = HALVES[1]
    send(("y", 4), wall.at[2, z, pl.ds(start, size)], wall.at[3, z, pl.ds(start, size)], y_prev)
    ring_step(1, 2)
    forward("k", kbuf)
    ring_step(1, 3)
    ring_step(2, 1)
    ring_step(1, 4)
    forward("v", vbuf)
    ring_step(2, 2)
    bias = key_bias()
    attention_wait()
    for h in range(heads):
        attention_head(h, bias)
        if h == 2:
            ring_step(2, 3)
    send("attn", attn.at[core], attn.at[core], sibling)
    for half in range(2):
        start, size = HALVES[half]
        receive(("y", 3 + half), wall.at[3, z, pl.ds(start, size)])
    ring_step(3, 1)
    ring_step(2, 4)
    ring_last(0)
    receive("attn", attn.at[1 - core])
    project(0)
    ring_step(3, 2)
    ring_last(1)
    project(1)
    reduce_x(0)
    ring_step(3, 3)
    ring_last(2)
    project(2)
    reduce_x(1)
    finish(0)
    ring_step(3, 4)
    reduce_x(2)
    finish(1)
    ring_last(3)
    project(3)
    finish(2)
    reduce_x(3)
    finish(3)
    for copy in started:
        copy.wait_send()


def on_device(q_heads, k_heads, v_heads, out_weight, out_gate, tile_map, key_tiles, key_count):
    tokens, width = q_heads.shape
    wcols = out_weight.shape[1]
    features = out_gate.shape[0]
    vmem = pl.BlockSpec(memory_space=pltpu.VMEM)
    smem = pl.BlockSpec(memory_space=pltpu.SMEM)
    bf16 = jnp.bfloat16
    return pl.pallas_call(
        kernel,
        out_shape=jax.ShapeDtypeStruct((features, tokens), bf16),
        in_specs=[vmem] * 5 + [smem] * 3,
        out_specs=vmem,
        scratch_shapes=[
            pltpu.VMEM((6, TILE, width), bf16),
            pltpu.VMEM((6, TILE, width), bf16),
            pltpu.VMEM((4, NZ, wcols, width), bf16),
            pltpu.VMEM((2, TILE, width), bf16),
            pltpu.VMEM((4, NX, NYL, wcols, 2 * TILE), bf16),
            pltpu.VMEM((4, NX - 1, NYL, wcols, 2 * TILE), bf16),
            pltpu.VMEM((4, NYL, 2, wcols, TILE), bf16),
            pltpu.VMEM((4, 3, wcols, TILE), bf16),
            pltpu.VMEM((features, HD), jnp.float32),
            pltpu.SemaphoreType.DMA((104,)),
            pltpu.SemaphoreType.DMA((104,)),
        ],
        compiler_params=pltpu.CompilerParams(
            collective_id=0, has_side_effects=True, vmem_limit_bytes=32 * 2**20
        ),
        cost_estimate=pl.CostEstimate(
            flops=1_100_000_000, bytes_accessed=2_000_000, transcendentals=500_000
        ),
        name="attend_project",
    )(q_heads, k_heads, v_heads, out_weight.T, out_gate.reshape(1, features),
      tile_map, key_tiles, key_count)


def solution(mesh):
    return jax.shard_map(
        on_device,
        mesh=mesh,
        in_specs=(
            P("seq", "fsdp"),
            P("seq", "fsdp"),
            P("seq", "fsdp"),
            P("fsdp", "seq"),
            P("fsdp"),
            P(),
            P(),
            P(),
        ),
        out_specs=P("fsdp", "seq"),
        check_vma=False,
    )
```

```python
import functools
import jax
import jax.numpy as jnp
from jax import lax
from jax.experimental import pallas as pl
from jax.experimental.pallas import tpu as pltpu
from jax.sharding import PartitionSpec as P

HD = 128
TILE = 128
KMAX = 4
NX, NYL, NZ, NYH = 4, 2, 8, 4
PLANES = NZ * NYH
NEG = -1e30
HALVES = ((0, 48), (48, 32))
MESH = pl.DeviceIdType.MESH


FEW = (1, 1)
ORDER = (2, 6, 1, 7, 3, 5, 4)
CHUNKS = ((0, 3), (3, 2))
OFFSETS = ((0, 0), (-1, 1), (1, -1), (2, 2))


def kernel(
    q_ref, k_ref, v_ref, w_ref, gate_ref, map_ref, list_ref, count_ref, out_ref,
    qbuf, kv, wtmp, wall, attn, toks, keep, give, take, sbuf, rbuf, gline, gcol,
    tile_map, key_list, key_count, local_sems, send_sems, recv_sems,
):
    heads = q_ref.shape[1] // HD
    wcols = w_ref.shape[0]
    f = lax.axis_index("fsdp")
    s = lax.axis_index("seq")
    yl, x = f // NX, f % NX
    core, yh, z = s % 2, (s // 2) % NYH, s // 8
    plane = s // 2

    def seq_id(zz, yy, cc):
        return zz * 8 + yy * 2 + cc

    def wrap(a, n):
        return (a + n) % n

    sibling = (f, seq_id(z, yh, 1 - core))
    z_next = (f, seq_id(wrap(z + 1, NZ), yh, core))
    z_prev = (f, seq_id(wrap(z - 1, NZ), yh, core))
    y_next = (f, seq_id(z, wrap(yh + 1, NYH), core))
    y_prev = (f, seq_id(z, wrap(yh - 1, NYH), core))
    p_next = (f, wrap(plane + 1, PLANES) * 2 + core)
    p_prev = (f, wrap(plane - 1, PLANES) * 2 + core)
    kind = ((x + 1) // 2) % 2
    own = core == kind
    mate = yl * NX + x + 1 - 2 * (x % 2)
    swap_peer = (mate, seq_id(z, yh, 1 - core))
    mate_core = (mate, seq_id(z, yh, kind))
    groups = NX * NYL
    fsdp_peer = [(wrap(f + r, groups), s) for r in range(groups)]

    peers = [sibling, z_next, z_prev, y_next, y_prev, p_next, p_prev, swap_peer] + fsdp_peer[1:]
    local = [
        pltpu.make_async_copy(src, dst, local_sems.at[n])
        for n, (src, dst) in enumerate((
            (w_ref, wtmp), (k_ref, kv.at[0, 0]), (v_ref, kv.at[0, 1]), (q_ref, qbuf),
            (gate_ref, gline), (map_ref, tile_map), (list_ref, key_list), (count_ref, key_count),
        ))
    ]
    for copy in local:
        copy.start()
    barrier = pltpu.get_barrier_semaphore()
    for peer in peers:
        pl.semaphore_signal(barrier, inc=1, device_id=peer, device_id_type=MESH)

    def gate_column():
        local[4].wait()
        rows = lax.broadcasted_iota(jnp.int32, (HD, HD), 0)
        cols = lax.broadcasted_iota(jnp.int32, (HD, HD), 1)
        for i in range(gline.shape[0] // HD):
            line = jnp.broadcast_to(gline[i * HD:(i + 1) * HD].reshape(1, HD), (HD, HD))
            column = jnp.sum(jnp.where(rows == cols, line, 0.0), axis=1, keepdims=True)
            gcol[i * HD:(i + 1) * HD, :] = jnp.broadcast_to(column, (HD, HD))

    for copy in local[:4]:
        copy.wait()
    pl.semaphore_wait(barrier, len(peers))

    started = []
    table = {}

    def number(key):
        return table.setdefault(key, len(table))

    def send(key, src, dst, peer):
        n = number(key)
        copy = pltpu.make_async_remote_copy(
            src_ref=src, dst_ref=dst, send_sem=send_sems.at[n], recv_sem=recv_sems.at[n],
            device_id=peer, device_id_type=MESH,
        )
        copy.start()
        started.append(copy)

    def receive(key, dst):
        n = number(key)
        pltpu.make_async_remote_copy(
            src_ref=dst, dst_ref=dst, send_sem=send_sems.at[n], recv_sem=recv_sems.at[n],
            device_id=sibling, device_id_type=MESH,
        ).wait_recv()

    def swap():
        n = number("swap")
        copy = pltpu.make_async_remote_copy(
            src_ref=wtmp, dst_ref=wall.at[0, z], send_sem=send_sems.at[n],
            recv_sem=recv_sems.at[n], device_id=swap_peer, device_id_type=MESH,
        )

        @pl.when(own)
        def _():
            wall[0, z] = wtmp[...]

        @pl.when(jnp.logical_not(own))
        def _():
            copy.start()
            copy.wait()

    def part(piece, zz, half):
        start, size = HALVES[half]
        return wall.at[piece, zz, pl.ds(start, size)]

    def ring_pieces(hop):
        return (wrap(z - hop, NZ), wrap(z + hop, NZ))

    def last_way(piece, half):
        inner = (piece + half) % 2
        low, high = (0, 1) if (piece, half) == FEW else (1, 0)
        return jnp.where(yh == 0, low, jnp.where(yh == NYH - 1, high, inner))

    def ring_step(piece, hop):
        for half in range(2):
            if hop > 1:
                for way, zz in enumerate(ring_pieces(hop - 1)):
                    receive(("z", piece, half, way, hop - 1), part(piece, zz, half))
                    if hop < 4:
                        ref = part(piece, zz, half)
                        send(("z", piece, half, way, hop), ref, ref, (z_next, z_prev)[way])
            else:
                for way in range(2):
                    ref = part(piece, z, half)
                    send(("z", piece, half, way, 1), ref, ref, (z_next, z_prev)[way])
            if hop == 4:
                turn = 2 * last_way(piece, half) - 1
                ref = part(piece, wrap(z + 3 * turn, NZ), half)
                peer = (f, seq_id(wrap(z - turn, NZ), yh, core))
                send(("z", piece, half, 4), ref, ref, peer)

    def ring_last(piece, halves=(0, 1)):
        for half in halves:
            receive(("z", piece, half, 4), part(piece, wrap(z + 4, NZ), half))

    def rows(piece, half):
        return part(piece, z, half)

    def weights_out(piece):
        for half in range(2):
            peer = y_next if (half == 0) == (piece == 1) else y_prev
            send(("y", piece, half), rows(0, half), rows(piece, half), peer)

    def weights_in(piece):
        for half in range(2):
            receive(("y", piece, half), rows(piece, half))

    def weights_on():
        for half, peer in ((0, y_next), (1, y_prev)):
            send(("y", 3, half), rows(1, half), rows(3, half), peer)

    def sibling_out():
        send(("s",), kv.at[0], kv.at[1], sibling)

    def heads_of(slot, chunk):
        start, size = CHUNKS[chunk]
        return kv.at[slot, :, :, pl.ds(start * HD, size * HD)]

    def halo(chunk):
        send(("h", chunk, 0), heads_of(0, chunk), heads_of(2, chunk), p_next)
        send(("h", chunk, 1), heads_of(0, chunk), heads_of(4, chunk), p_prev)

    def forward(chunk):
        for way, slot in ((0, 2), (1, 4)):
            receive(("h", chunk, way), heads_of(slot, chunk))
            send(("g", chunk, way), heads_of(slot, chunk), heads_of(slot + 1, chunk), sibling)

    def key_bias():
        for copy in local[5:]:
            copy.wait()
        tile = tile_map[s]
        used = key_count[tile]
        listed = [key_list[i, tile] for i in range(KMAX)]
        below, above = wrap(plane - 1, PLANES), wrap(plane + 1, PLANES)
        slots = (
            (s, None), (plane * 2 + 1 - core, None),
            (below * 2 + core, plane > 0), (below * 2 + 1 - core, plane > 0),
            (above * 2 + core, plane < PLANES - 1), (above * 2 + 1 - core, plane < PLANES - 1),
        )
        lane_tile = lax.broadcasted_iota(jnp.int32, (1, 6 * TILE), 1) // TILE
        bias = jnp.zeros((1, 6 * TILE), jnp.float32)
        for n, (slot, inside) in enumerate(slots):
            other = tile_map[slot]
            hit = jnp.int32(0)
            for i in range(KMAX):
                same = jnp.where(listed[i] == other, 1, 0) * jnp.where(used > i, 1, 0)
                hit = jnp.maximum(hit, same)
            if inside is not None:
                hit = hit * jnp.where(inside, 1, 0)
            value = jnp.where(hit == 1, 0.0, NEG).astype(jnp.float32)
            bias = jnp.where(lane_tile == n, value, bias)
        return bias

    def attention_head(h, bias):
        span = slice(h * HD, (h + 1) * HD)
        keys = kv[:, 0, :, span].reshape(6 * TILE, HD)
        values = kv[:, 1, :, span].reshape(6 * TILE, HD)
        scores = lax.dot_general(
            qbuf[:, span], keys, (((1,), (1,)), ((), ())), preferred_element_type=jnp.float32
        )
        scores = scores * (1.0 / float(HD) ** 0.5) + bias
        top = jnp.max(scores, axis=1, keepdims=True)
        expo = jnp.exp(scores - top)
        total = jnp.sum(expo, axis=1, keepdims=True)
        mixed = jnp.dot(expo.astype(jnp.bfloat16), values, preferred_element_type=jnp.float32)
        attn[:, span] = (mixed / total).astype(jnp.bfloat16)

    def token_copy(name, chunk, slot, peer):
        n, m = number(("a", name, chunk)), number(("a", slot, chunk))
        start, size = CHUNKS[chunk]
        span = pl.ds(start * HD, size * HD)
        return pltpu.make_async_remote_copy(
            src_ref=attn.at[:, span], dst_ref=toks.at[slot, :, span], send_sem=send_sems.at[n],
            recv_sem=recv_sems.at[m], device_id=peer, device_id_type=MESH,
        )

    def attention(chunk, bias):
        for way, slot in ((0, 3), (1, 5)):
            receive(("g", chunk, way), heads_of(slot, chunk))
        start, size = CHUNKS[chunk]
        for h in range(start, start + size):
            attention_head(h, bias)

        @pl.when(own)
        def _():
            token_copy("mate", chunk, 0, mate_core).start()
            span = slice(start * HD, (start + size) * HD)
            toks[0, :, span] = attn[:, span]

        @pl.when(jnp.logical_not(own))
        def _():
            token_copy("mate", chunk, 1, mate_core).start()
            token_copy("sib", chunk, 1, sibling).start()

    def tokens_in(chunk):
        @pl.when(jnp.logical_not(own))
        def _():
            token_copy(0, chunk, 0, sibling).wait_recv()

        token_copy(1, chunk, 1, sibling).wait_recv()

    def tokens_end(chunk):
        token_copy("mate", chunk, 1, mate_core).wait_send()

        @pl.when(jnp.logical_not(own))
        def _():
            token_copy("sib", chunk, 1, sibling).wait_send()

    def span_of(half):
        return (0, wcols) if half is None else HALVES[half]

    def project(piece, half=None):
        start, size = span_of(half)
        span = pl.ds(start, size)
        weights = wall[piece, :, span].reshape(NZ * size, heads * HD)
        tokens = toks[...].reshape(2 * TILE, heads * HD)
        partial = lax.dot_general(
            weights, tokens, (((1,), (1,)), ((), ())), preferred_element_type=jnp.float32
        )
        give[piece, :, span] = partial[:, TILE:].astype(jnp.bfloat16).reshape(NZ, size, TILE)
        send(("c", piece, half), give.at[piece, :, span], take.at[piece, :, span], sibling)
        keep[piece, :, span] = partial[:, :TILE].reshape(NZ, size, TILE)

    def scatter(piece, half=None):
        start, size = span_of(half)
        span = pl.ds(start, size)
        receive(("c", piece, half), take.at[piece, :, span])
        total = keep[piece, :, span] + take[piece, :, span].astype(jnp.float32)
        sbuf[piece, :, span] = total.astype(jnp.bfloat16)
        for r in ORDER:
            dst = rbuf.at[piece, f, span]
            to = fsdp_peer[r]
            send(("f", piece, half, r), sbuf.at[piece, to[0], span], dst, to)
        rbuf[piece, f, span] = sbuf[piece, f, span]

    def finish(piece, half=None):
        start, size = span_of(half)
        span = pl.ds(start, size)
        for r in ORDER:
            receive(("f", piece, half, r), rbuf.at[piece, wrap(f - r, groups), span])
        for part_half in range(2) if half is None else (half,):
            start, size = HALVES[part_half]
            span = pl.ds(start, size)
            from_yh = wrap(yh + OFFSETS[piece][part_half], NYH)
            for column_core, sources in ((0, (0, 3, 4, 7)), (1, (1, 2, 5, 6))):
                first = pl.multiple_of(from_yh * (2 * wcols) + column_core * wcols + start, 16)
                summed = jnp.zeros((size, TILE), jnp.float32)
                for source in sources:
                    summed = summed + rbuf[piece, source, span].astype(jnp.float32)
                gate = gcol[pl.ds(first, size), :]
                out_ref[pl.ds(first, size), :] = (gate * summed).astype(out_ref.dtype)

    swap()
    weights_out(1)
    ring_step(0, 1)
    weights_out(2)
    sibling_out()
    gate_column()
    bias = key_bias()
    ring_step(0, 2)
    halo(0)
    weights_in(1)
    weights_on()
    ring_step(1, 1)
    ring_step(0, 3)
    halo(1)
    ring_step(1, 2)
    ring_step(0, 4)
    weights_in(2)
    ring_step(2, 1)
    ring_step(1, 3)
    ring_step(2, 2)
    ring_step(1, 4)
    weights_in(3)
    ring_step(3, 1)
    forward(0)
    ring_step(2, 3)
    receive(("s",), kv.at[1])
    attention(0, bias)
    ring_step(3, 2)
    forward(1)
    ring_step(2, 4)
    attention(1, bias)
    ring_step(3, 3)
    ring_last(0)
    tokens_in(0)
    tokens_in(1)
    project(0)
    ring_last(1)
    project(1)
    scatter(0)
    ring_step(3, 4)
    scatter(1)
    ring_last(2)
    project(2)
    finish(0)
    scatter(2)
    ring_last(3, (0,))
    project(3, 0)
    ring_last(3, (1,))
    project(3, 1)
    finish(1)
    scatter(3, 0)
    scatter(3, 1)
    finish(2)
    finish(3, 0)
    finish(3, 1)
    tokens_end(0)
    tokens_end(1)
    for copy in started:
        copy.wait_send()


def on_device(q_heads, k_heads, v_heads, out_weight, out_gate, tile_map, key_tiles, key_count):
    tokens, width = q_heads.shape
    wcols = out_weight.shape[1]
    features = out_gate.shape[0]
    vmem = pl.BlockSpec(memory_space=pltpu.VMEM)
    bf16 = jnp.bfloat16
    return pl.pallas_call(
        kernel,
        out_shape=jax.ShapeDtypeStruct((features, tokens), bf16),
        in_specs=[pl.BlockSpec(memory_space=pl.ANY)] * 8,
        out_specs=vmem,
        scratch_shapes=[
            pltpu.VMEM((TILE, width), bf16),
            pltpu.VMEM((6, 2, TILE, width), bf16),
            pltpu.VMEM((wcols, width), bf16),
            pltpu.VMEM((4, NZ, wcols, width), bf16),
            pltpu.VMEM((TILE, width), bf16),
            pltpu.VMEM((2, TILE, width), bf16),
            pltpu.VMEM((4, NZ, wcols, TILE), jnp.float32),
            pltpu.VMEM((4, NZ, wcols, TILE), bf16),
            pltpu.VMEM((4, NZ, wcols, TILE), bf16),
            pltpu.VMEM((4, NZ, wcols, TILE), bf16),
            pltpu.VMEM((4, NX * NYL, wcols, TILE), bf16),
            pltpu.VMEM((features,), jnp.float32),
            pltpu.VMEM((features, HD), jnp.float32),
            pltpu.SMEM(tile_map.shape, jnp.int32),
            pltpu.SMEM(key_tiles.shape[::-1], jnp.int32),
            pltpu.SMEM(key_count.shape, jnp.int32),
            pltpu.SemaphoreType.DMA((8,)),
            pltpu.SemaphoreType.DMA((128,)),
            pltpu.SemaphoreType.DMA((128,)),
        ],
        compiler_params=pltpu.CompilerParams(
            collective_id=0, has_side_effects=True, vmem_limit_bytes=56 * 2**20
        ),
        cost_estimate=pl.CostEstimate(
            flops=1_100_000_000, bytes_accessed=2_000_000, transcendentals=500_000
        ),
        name="attend_project",
    )(q_heads, k_heads, v_heads, out_weight.T, out_gate, tile_map, key_tiles.T, key_count)


def solution(mesh):
    return jax.shard_map(
        on_device,
        mesh=mesh,
        in_specs=(
            P("seq", "fsdp"),
            P("seq", "fsdp"),
            P("seq", "fsdp"),
            P("fsdp", "seq"),
            P("fsdp"),
            P(),
            P(),
            P(),
        ),
        out_specs=P("fsdp", "seq"),
        check_vma=False,
    )
```

```python
import functools
import jax
import jax.numpy as jnp
from jax import lax
from jax.experimental import pallas as pl
from jax.experimental.pallas import tpu as pltpu
from jax.sharding import PartitionSpec as P

HD = 128
TILE = 128
KMAX = 4
NX, NYL, NZ, NYH = 4, 2, 8, 4
PLANES = NZ * NYH
NEG = -1e30
HALVES = ((0, 48), (48, 32))
MESH = pl.DeviceIdType.MESH


FEW = (1, 1)
ORDER = (2, 6, 1, 7, 3, 5, 4)
CHUNKS = ((0, 3), (3, 2))
OFFSETS = ((0, 0), (-1, 1), (1, -1), (2, 2))


def kernel(
    q_ref, k_ref, v_ref, w_ref, gate_ref, map_ref, list_ref, count_ref, out_ref,
    qbuf, kv, wtmp, wall, attn, toks, keep, give, take, sbuf, rbuf, gline, gcol,
    tile_map, key_list, key_count, obuf, out_sems, local_sems, send_sems, recv_sems,
):
    heads = q_ref.shape[1] // HD
    wcols = w_ref.shape[0]
    f = lax.axis_index("fsdp")
    s = lax.axis_index("seq")
    yl, x = f // NX, f % NX
    core, yh, z = s % 2, (s // 2) % NYH, s // 8
    plane = s // 2

    def seq_id(zz, yy, cc):
        return zz * 8 + yy * 2 + cc

    def wrap(a, n):
        return (a + n) % n

    sibling = (f, seq_id(z, yh, 1 - core))
    z_next = (f, seq_id(wrap(z + 1, NZ), yh, core))
    z_prev = (f, seq_id(wrap(z - 1, NZ), yh, core))
    y_next = (f, seq_id(z, wrap(yh + 1, NYH), core))
    y_prev = (f, seq_id(z, wrap(yh - 1, NYH), core))
    p_next = (f, wrap(plane + 1, PLANES) * 2 + core)
    p_prev = (f, wrap(plane - 1, PLANES) * 2 + core)
    kind = ((x + 1) // 2) % 2
    own = core == kind
    mate = yl * NX + x + 1 - 2 * (x % 2)
    swap_peer = (mate, seq_id(z, yh, 1 - core))
    mate_core = (mate, seq_id(z, yh, kind))
    groups = NX * NYL
    fsdp_peer = [(wrap(f + r, groups), s) for r in range(groups)]

    peers = [sibling, z_next, z_prev, y_next, y_prev, p_next, p_prev, swap_peer] + fsdp_peer[1:]
    local = [
        pltpu.make_async_copy(src, dst, local_sems.at[n])
        for n, (src, dst) in enumerate((
            (w_ref, wtmp), (k_ref, kv.at[0, 0]), (v_ref, kv.at[0, 1]), (q_ref, qbuf),
            (gate_ref, gline), (map_ref, tile_map), (list_ref, key_list), (count_ref, key_count),
        ))
    ]
    for copy in local:
        copy.start()
    barrier = pltpu.get_barrier_semaphore()
    for peer in peers:
        pl.semaphore_signal(barrier, inc=1, device_id=peer, device_id_type=MESH)

    def gate_column():
        local[4].wait()
        rows = lax.broadcasted_iota(jnp.int32, (HD, HD), 0)
        cols = lax.broadcasted_iota(jnp.int32, (HD, HD), 1)
        for i in range(gline.shape[0] // HD):
            line = jnp.broadcast_to(gline[i * HD:(i + 1) * HD].reshape(1, HD), (HD, HD))
            column = jnp.sum(jnp.where(rows == cols, line, 0.0), axis=1, keepdims=True)
            gcol[i * HD:(i + 1) * HD, :] = jnp.broadcast_to(column, (HD, HD))

    for copy in local[:4]:
        copy.wait()
    pl.semaphore_wait(barrier, len(peers))

    started = []
    written = []
    table = {}

    def number(key):
        return table.setdefault(key, len(table))

    def send(key, src, dst, peer):
        n = number(key)
        copy = pltpu.make_async_remote_copy(
            src_ref=src, dst_ref=dst, send_sem=send_sems.at[n], recv_sem=recv_sems.at[n],
            device_id=peer, device_id_type=MESH,
        )
        copy.start()
        started.append(copy)

    def receive(key, dst):
        n = number(key)
        pltpu.make_async_remote_copy(
            src_ref=dst, dst_ref=dst, send_sem=send_sems.at[n], recv_sem=recv_sems.at[n],
            device_id=sibling, device_id_type=MESH,
        ).wait_recv()

    def swap():
        n = number("swap")
        copy = pltpu.make_async_remote_copy(
            src_ref=wtmp, dst_ref=wall.at[0, z], send_sem=send_sems.at[n],
            recv_sem=recv_sems.at[n], device_id=swap_peer, device_id_type=MESH,
        )

        @pl.when(own)
        def _():
            wall[0, z] = wtmp[...]

        @pl.when(jnp.logical_not(own))
        def _():
            copy.start()
            copy.wait()

    def part(piece, zz, half):
        start, size = HALVES[half]
        return wall.at[piece, zz, pl.ds(start, size)]

    def ring_pieces(hop):
        return (wrap(z - hop, NZ), wrap(z + hop, NZ))

    def last_way(piece, half):
        inner = (piece + half) % 2
        low, high = (0, 1) if (piece, half) == FEW else (1, 0)
        return jnp.where(yh == 0, low, jnp.where(yh == NYH - 1, high, inner))

    def ring_step(piece, hop):
        for half in range(2):
            if hop > 1:
                for way, zz in enumerate(ring_pieces(hop - 1)):
                    receive(("z", piece, half, way, hop - 1), part(piece, zz, half))
                    if hop < 4:
                        ref = part(piece, zz, half)
                        send(("z", piece, half, way, hop), ref, ref, (z_next, z_prev)[way])
            else:
                for way in range(2):
                    ref = part(piece, z, half)
                    send(("z", piece, half, way, 1), ref, ref, (z_next, z_prev)[way])
            if hop == 4:
                turn = 2 * last_way(piece, half) - 1
                ref = part(piece, wrap(z + 3 * turn, NZ), half)
                peer = (f, seq_id(wrap(z - turn, NZ), yh, core))
                send(("z", piece, half, 4), ref, ref, peer)

    def ring_last(piece, halves=(0, 1)):
        for half in halves:
            receive(("z", piece, half, 4), part(piece, wrap(z + 4, NZ), half))

    def rows(piece, half):
        return part(piece, z, half)

    def weights_out(piece):
        for half in range(2):
            peer = y_next if (half == 0) == (piece == 1) else y_prev
            send(("y", piece, half), rows(0, half), rows(piece, half), peer)

    def weights_in(piece):
        for half in range(2):
            receive(("y", piece, half), rows(piece, half))

    def weights_on():
        for half, peer in ((0, y_next), (1, y_prev)):
            send(("y", 3, half), rows(1, half), rows(3, half), peer)

    def sibling_out():
        send(("s",), kv.at[0], kv.at[1], sibling)

    def heads_of(slot, chunk):
        start, size = CHUNKS[chunk]
        return kv.at[slot, :, :, pl.ds(start * HD, size * HD)]

    def halo(chunk):
        send(("h", chunk, 0), heads_of(0, chunk), heads_of(2, chunk), p_next)
        send(("h", chunk, 1), heads_of(0, chunk), heads_of(4, chunk), p_prev)

    def forward(chunk):
        for way, slot in ((0, 2), (1, 4)):
            receive(("h", chunk, way), heads_of(slot, chunk))
            send(("g", chunk, way), heads_of(slot, chunk), heads_of(slot + 1, chunk), sibling)

    def key_bias():
        for copy in local[5:]:
            copy.wait()
        tile = tile_map[s]
        used = key_count[tile]
        listed = [key_list[i, tile] for i in range(KMAX)]
        below, above = wrap(plane - 1, PLANES), wrap(plane + 1, PLANES)
        slots = (
            (s, None), (plane * 2 + 1 - core, None),
            (below * 2 + core, plane > 0), (below * 2 + 1 - core, plane > 0),
            (above * 2 + core, plane < PLANES - 1), (above * 2 + 1 - core, plane < PLANES - 1),
        )
        lane_tile = lax.broadcasted_iota(jnp.int32, (1, 6 * TILE), 1) // TILE
        bias = jnp.zeros((1, 6 * TILE), jnp.float32)
        for n, (slot, inside) in enumerate(slots):
            other = tile_map[slot]
            hit = jnp.int32(0)
            for i in range(KMAX):
                same = jnp.where(listed[i] == other, 1, 0) * jnp.where(used > i, 1, 0)
                hit = jnp.maximum(hit, same)
            if inside is not None:
                hit = hit * jnp.where(inside, 1, 0)
            value = jnp.where(hit == 1, 0.0, NEG).astype(jnp.float32)
            bias = jnp.where(lane_tile == n, value, bias)
        return bias

    def attention_head(h, bias):
        span = slice(h * HD, (h + 1) * HD)
        keys = kv[:, 0, :, span].reshape(6 * TILE, HD)
        values = kv[:, 1, :, span].reshape(6 * TILE, HD)
        scores = lax.dot_general(
            qbuf[:, span], keys, (((1,), (1,)), ((), ())), preferred_element_type=jnp.float32
        )
        scores = scores * (1.0 / float(HD) ** 0.5) + bias
        top = jnp.max(scores, axis=1, keepdims=True)
        expo = jnp.exp(scores - top)
        total = jnp.sum(expo, axis=1, keepdims=True)
        mixed = jnp.dot(expo.astype(jnp.bfloat16), values, preferred_element_type=jnp.float32)
        attn[:, span] = (mixed / total).astype(jnp.bfloat16)

    def token_copy(name, chunk, slot, peer):
        n, m = number(("a", name, chunk)), number(("a", slot, chunk))
        start, size = CHUNKS[chunk]
        span = pl.ds(start * HD, size * HD)
        return pltpu.make_async_remote_copy(
            src_ref=attn.at[:, span], dst_ref=toks.at[slot, :, span], send_sem=send_sems.at[n],
            recv_sem=recv_sems.at[m], device_id=peer, device_id_type=MESH,
        )

    def attention(chunk, bias):
        for way, slot in ((0, 3), (1, 5)):
            receive(("g", chunk, way), heads_of(slot, chunk))
        start, size = CHUNKS[chunk]
        for h in range(start, start + size):
            attention_head(h, bias)

        @pl.when(own)
        def _():
            token_copy("mate", chunk, 0, mate_core).start()
            span = slice(start * HD, (start + size) * HD)
            toks[0, :, span] = attn[:, span]

        @pl.when(jnp.logical_not(own))
        def _():
            token_copy("mate", chunk, 1, mate_core).start()
            token_copy("sib", chunk, 1, sibling).start()

    def tokens_in(chunk):
        @pl.when(jnp.logical_not(own))
        def _():
            token_copy(0, chunk, 0, sibling).wait_recv()

        token_copy(1, chunk, 1, sibling).wait_recv()

    def tokens_end(chunk):
        token_copy("mate", chunk, 1, mate_core).wait_send()

        @pl.when(jnp.logical_not(own))
        def _():
            token_copy("sib", chunk, 1, sibling).wait_send()

    def span_of(half):
        return (0, wcols) if half is None else HALVES[half]

    def project(piece, half=None):
        start, size = span_of(half)
        span = pl.ds(start, size)
        weights = wall[piece, :, span].reshape(NZ * size, heads * HD)
        tokens = toks[...].reshape(2 * TILE, heads * HD)
        partial = lax.dot_general(
            weights, tokens, (((1,), (1,)), ((), ())), preferred_element_type=jnp.float32
        )
        give[piece, :, span] = partial[:, TILE:].astype(jnp.bfloat16).reshape(NZ, size, TILE)
        send(("c", piece, half), give.at[piece, :, span], take.at[piece, :, span], sibling)
        keep[piece, :, span] = partial[:, :TILE].reshape(NZ, size, TILE)

    def scatter(piece, half=None):
        start, size = span_of(half)
        span = pl.ds(start, size)
        receive(("c", piece, half), take.at[piece, :, span])
        total = keep[piece, :, span] + take[piece, :, span].astype(jnp.float32)
        sbuf[piece, :, span] = total.astype(jnp.bfloat16)
        for r in ORDER:
            dst = rbuf.at[piece, f, span]
            to = fsdp_peer[r]
            send(("f", piece, half, r), sbuf.at[piece, to[0], span], dst, to)
        rbuf[piece, f, span] = sbuf[piece, f, span]

    def finish(piece, half=None):
        start, size = span_of(half)
        span = pl.ds(start, size)
        for r in ORDER:
            receive(("f", piece, half, r), rbuf.at[piece, wrap(f - r, groups), span])
        for part_half in range(2) if half is None else (half,):
            start, size = HALVES[part_half]
            span = pl.ds(start, size)
            from_yh = wrap(yh + OFFSETS[piece][part_half], NYH)
            for column_core, sources in ((0, (0, 3, 4, 7)), (1, (1, 2, 5, 6))):
                first = pl.multiple_of(from_yh * (2 * wcols) + column_core * wcols + start, 16)
                summed = jnp.zeros((size, TILE), jnp.float32)
                for source in sources:
                    summed = summed + rbuf[piece, source, span].astype(jnp.float32)
                gate = gcol[pl.ds(first, size), :]
                obuf[pl.ds(first, size), :] = (gate * summed).astype(obuf.dtype)
                out = pltpu.make_async_copy(
                    obuf.at[pl.ds(first, size)], out_ref.at[pl.ds(first, size)],
                    out_sems.at[(piece * 2 + part_half) * 2 + column_core],
                )
                out.start()
                written.append(out)

    swap()
    weights_out(1)
    ring_step(0, 1)
    weights_out(2)
    sibling_out()
    gate_column()
    bias = key_bias()
    receive(("s",), kv.at[1])
    ring_step(0, 2)
    halo(0)
    weights_in(1)
    weights_on()
    ring_step(1, 1)
    ring_step(0, 3)
    halo(1)
    ring_step(1, 2)
    ring_step(0, 4)
    weights_in(2)
    ring_step(2, 1)
    ring_step(1, 3)
    ring_step(2, 2)
    ring_step(1, 4)
    forward(0)
    weights_in(3)
    ring_step(3, 1)
    attention(0, bias)
    ring_step(2, 3)
    forward(1)
    ring_step(3, 2)
    attention(1, bias)
    ring_step(2, 4)
    ring_step(3, 3)
    ring_last(0)
    tokens_in(0)
    tokens_in(1)
    project(0)
    ring_last(1)
    project(1)
    scatter(0)
    ring_step(3, 4)
    scatter(1)
    ring_last(2)
    project(2)
    finish(0)
    scatter(2)
    ring_last(3, (0,))
    project(3, 0)
    ring_last(3, (1,))
    project(3, 1)
    finish(1)
    scatter(3, 0)
    scatter(3, 1)
    finish(2)
    finish(3, 0)
    finish(3, 1)
    tokens_end(0)
    tokens_end(1)
    for copy in started:
        copy.wait_send()
    for copy in written:
        copy.wait()


def on_device(q_heads, k_heads, v_heads, out_weight, out_gate, tile_map, key_tiles, key_count):
    tokens, width = q_heads.shape
    wcols = out_weight.shape[1]
    features = out_gate.shape[0]
    bf16 = jnp.bfloat16
    return pl.pallas_call(
        kernel,
        out_shape=jax.ShapeDtypeStruct((features, tokens), bf16),
        in_specs=[pl.BlockSpec(memory_space=pl.ANY)] * 8,
        out_specs=pl.BlockSpec(memory_space=pl.ANY),
        scratch_shapes=[
            pltpu.VMEM((TILE, width), bf16),
            pltpu.VMEM((6, 2, TILE, width), bf16),
            pltpu.VMEM((wcols, width), bf16),
            pltpu.VMEM((4, NZ, wcols, width), bf16),
            pltpu.VMEM((TILE, width), bf16),
            pltpu.VMEM((2, TILE, width), bf16),
            pltpu.VMEM((4, NZ, wcols, TILE), jnp.float32),
            pltpu.VMEM((4, NZ, wcols, TILE), bf16),
            pltpu.VMEM((4, NZ, wcols, TILE), bf16),
            pltpu.VMEM((4, NZ, wcols, TILE), bf16),
            pltpu.VMEM((4, NX * NYL, wcols, TILE), bf16),
            pltpu.VMEM((features,), jnp.float32),
            pltpu.VMEM((features, HD), jnp.float32),
            pltpu.SMEM(tile_map.shape, jnp.int32),
            pltpu.SMEM(key_tiles.shape[::-1], jnp.int32),
            pltpu.SMEM(key_count.shape, jnp.int32),
            pltpu.VMEM((features, tokens), bf16),
            pltpu.SemaphoreType.DMA((16,)),
            pltpu.SemaphoreType.DMA((8,)),
            pltpu.SemaphoreType.DMA((128,)),
            pltpu.SemaphoreType.DMA((128,)),
        ],
        compiler_params=pltpu.CompilerParams(
            collective_id=0, has_side_effects=True, vmem_limit_bytes=56 * 2**20
        ),
        cost_estimate=pl.CostEstimate(
            flops=1_100_000_000, bytes_accessed=2_000_000, transcendentals=500_000
        ),
        name="attend_project",
    )(q_heads, k_heads, v_heads, out_weight.T, out_gate, tile_map, key_tiles.T, key_count)


def solution(mesh):
    return jax.shard_map(
        on_device,
        mesh=mesh,
        in_specs=(
            P("seq", "fsdp"),
            P("seq", "fsdp"),
            P("seq", "fsdp"),
            P("fsdp", "seq"),
            P("fsdp"),
            P(),
            P(),
            P(),
        ),
        out_specs=P("fsdp", "seq"),
        check_vma=False,
    )
```

```python
import functools
import jax
import jax.numpy as jnp
from jax import lax
from jax.experimental import pallas as pl
from jax.experimental.pallas import tpu as pltpu
from jax.sharding import PartitionSpec as P

HD = 128
TILE = 128
KMAX = 4
NX, NYL, NZ, NYH = 4, 2, 8, 4
PLANES = NZ * NYH
NEG = -1e30
HALVES = ((0, 48), (48, 32))
MESH = pl.DeviceIdType.MESH


FEW = (1, 1)
ORDER = (2, 6, 1, 7, 3, 5, 4)
CHUNKS = ((0, 3), (3, 2))
OFFSETS = ((0, 0), (-1, 1), (1, -1), (2, 2))


def kernel(
    q_ref, k_ref, v_ref, w_ref, gate_ref, map_ref, list_ref, count_ref, out_ref,
    qbuf, kv, wtmp, wall, attn, toks, keep, give, take, sbuf, rbuf, gline, gcol,
    tile_map, key_list, key_count, obuf, out_sems, local_sems, send_sems, recv_sems,
):
    heads = q_ref.shape[1] // HD
    wcols = w_ref.shape[0]
    f = lax.axis_index("fsdp")
    s = lax.axis_index("seq")
    yl, x = f // NX, f % NX
    core, yh, z = s % 2, (s // 2) % NYH, s // 8
    plane = s // 2

    def seq_id(zz, yy, cc):
        return zz * 8 + yy * 2 + cc

    def wrap(a, n):
        return (a + n) % n

    sibling = (f, seq_id(z, yh, 1 - core))
    z_next = (f, seq_id(wrap(z + 1, NZ), yh, core))
    z_prev = (f, seq_id(wrap(z - 1, NZ), yh, core))
    y_next = (f, seq_id(z, wrap(yh + 1, NYH), core))
    y_prev = (f, seq_id(z, wrap(yh - 1, NYH), core))
    p_next = (f, wrap(plane + 1, PLANES) * 2 + core)
    p_prev = (f, wrap(plane - 1, PLANES) * 2 + core)
    kind = ((x + 1) // 2) % 2
    own = core == kind
    mate = yl * NX + x + 1 - 2 * (x % 2)
    swap_peer = (mate, seq_id(z, yh, 1 - core))
    mate_core = (mate, seq_id(z, yh, kind))
    groups = NX * NYL
    fsdp_peer = [(wrap(f + r, groups), s) for r in range(groups)]

    peers = [sibling, z_next, z_prev, y_next, y_prev, p_next, p_prev, swap_peer] + fsdp_peer[1:]
    local = [
        pltpu.make_async_copy(src, dst, local_sems.at[n])
        for n, (src, dst) in enumerate((
            (w_ref, wtmp), (k_ref, kv.at[0, 0]), (v_ref, kv.at[0, 1]), (q_ref, qbuf),
            (gate_ref, gline), (map_ref, tile_map), (list_ref, key_list), (count_ref, key_count),
        ))
    ]
    for copy in local:
        copy.start()
    barrier = pltpu.get_barrier_semaphore()
    for peer in peers:
        pl.semaphore_signal(barrier, inc=1, device_id=peer, device_id_type=MESH)

    def gate_column():
        local[4].wait()
        rows = lax.broadcasted_iota(jnp.int32, (HD, HD), 0)
        cols = lax.broadcasted_iota(jnp.int32, (HD, HD), 1)
        for i in range(gline.shape[0] // HD):
            line = jnp.broadcast_to(gline[i * HD:(i + 1) * HD].reshape(1, HD), (HD, HD))
            column = jnp.sum(jnp.where(rows == cols, line, 0.0), axis=1, keepdims=True)
            gcol[i * HD:(i + 1) * HD, :] = jnp.broadcast_to(column, (HD, HD))

    for copy in local[:4]:
        copy.wait()
    pl.semaphore_wait(barrier, len(peers))

    started = []
    written = []
    table = {}

    def number(key):
        return table.setdefault(key, len(table))

    def send(key, src, dst, peer):
        n = number(key)
        copy = pltpu.make_async_remote_copy(
            src_ref=src, dst_ref=dst, send_sem=send_sems.at[n], recv_sem=recv_sems.at[n],
            device_id=peer, device_id_type=MESH,
        )
        copy.start()
        started.append(copy)

    def receive(key, dst):
        n = number(key)
        pltpu.make_async_remote_copy(
            src_ref=dst, dst_ref=dst, send_sem=send_sems.at[n], recv_sem=recv_sems.at[n],
            device_id=sibling, device_id_type=MESH,
        ).wait_recv()

    def swap():
        n = number("swap")
        copy = pltpu.make_async_remote_copy(
            src_ref=wtmp, dst_ref=wall.at[0, z], send_sem=send_sems.at[n],
            recv_sem=recv_sems.at[n], device_id=swap_peer, device_id_type=MESH,
        )

        @pl.when(own)
        def _():
            wall[0, z] = wtmp[...]

        @pl.when(jnp.logical_not(own))
        def _():
            copy.start()
            copy.wait()

    def part(piece, zz, half):
        start, size = HALVES[half]
        return wall.at[piece, zz, pl.ds(start, size)]

    def ring_pieces(hop):
        return (wrap(z - hop, NZ), wrap(z + hop, NZ))

    def last_way(piece, half):
        inner = (piece + half) % 2
        low, high = (0, 1) if (piece, half) == FEW else (1, 0)
        return jnp.where(yh == 0, low, jnp.where(yh == NYH - 1, high, inner))

    def ring_step(piece, hop):
        for half in range(2):
            if hop > 1:
                for way, zz in enumerate(ring_pieces(hop - 1)):
                    receive(("z", piece, half, way, hop - 1), part(piece, zz, half))
                    if hop < 4:
                        ref = part(piece, zz, half)
                        send(("z", piece, half, way, hop), ref, ref, (z_next, z_prev)[way])
            else:
                for way in range(2):
                    ref = part(piece, z, half)
                    send(("z", piece, half, way, 1), ref, ref, (z_next, z_prev)[way])
            if hop == 4:
                turn = 2 * last_way(piece, half) - 1
                ref = part(piece, wrap(z + 3 * turn, NZ), half)
                peer = (f, seq_id(wrap(z - turn, NZ), yh, core))
                send(("z", piece, half, 4), ref, ref, peer)

    def ring_last(piece, halves=(0, 1)):
        for half in halves:
            receive(("z", piece, half, 4), part(piece, wrap(z + 4, NZ), half))

    def rows(piece, half):
        return part(piece, z, half)

    def weights_out(piece):
        for half in range(2):
            peer = y_next if (half == 0) == (piece == 1) else y_prev
            send(("y", piece, half), rows(0, half), rows(piece, half), peer)

    def weights_in(piece):
        for half in range(2):
            receive(("y", piece, half), rows(piece, half))

    def weights_on():
        for half, peer in ((0, y_next), (1, y_prev)):
            send(("y", 3, half), rows(1, half), rows(3, half), peer)

    def sibling_out():
        send(("s",), kv.at[0], kv.at[1], sibling)

    def heads_of(slot, chunk):
        start, size = CHUNKS[chunk]
        return kv.at[slot, :, :, pl.ds(start * HD, size * HD)]

    def halo(chunk):
        send(("h", chunk, 0), heads_of(0, chunk), heads_of(2, chunk), p_next)
        send(("h", chunk, 1), heads_of(0, chunk), heads_of(4, chunk), p_prev)

    def forward(chunk):
        for way, slot in ((0, 2), (1, 4)):
            receive(("h", chunk, way), heads_of(slot, chunk))
            send(("g", chunk, way), heads_of(slot, chunk), heads_of(slot + 1, chunk), sibling)

    def key_bias():
        for copy in local[5:]:
            copy.wait()
        tile = tile_map[s]
        used = key_count[tile]
        listed = [key_list[i, tile] for i in range(KMAX)]
        below, above = wrap(plane - 1, PLANES), wrap(plane + 1, PLANES)
        slots = (
            (s, None), (plane * 2 + 1 - core, None),
            (below * 2 + core, plane > 0), (below * 2 + 1 - core, plane > 0),
            (above * 2 + core, plane < PLANES - 1), (above * 2 + 1 - core, plane < PLANES - 1),
        )
        lane_tile = lax.broadcasted_iota(jnp.int32, (1, 6 * TILE), 1) // TILE
        bias = jnp.zeros((1, 6 * TILE), jnp.float32)
        for n, (slot, inside) in enumerate(slots):
            other = tile_map[slot]
            hit = jnp.int32(0)
            for i in range(KMAX):
                same = jnp.where(listed[i] == other, 1, 0) * jnp.where(used > i, 1, 0)
                hit = jnp.maximum(hit, same)
            if inside is not None:
                hit = hit * jnp.where(inside, 1, 0)
            value = jnp.where(hit == 1, 0.0, NEG).astype(jnp.float32)
            bias = jnp.where(lane_tile == n, value, bias)
        return bias

    def attention_head(h, bias):
        span = slice(h * HD, (h + 1) * HD)
        keys = kv[:, 0, :, span].reshape(6 * TILE, HD)
        values = kv[:, 1, :, span].reshape(6 * TILE, HD)
        scores = lax.dot_general(
            qbuf[:, span], keys, (((1,), (1,)), ((), ())), preferred_element_type=jnp.float32
        )
        scores = scores * (1.0 / float(HD) ** 0.5) + bias
        top = jnp.max(scores, axis=1, keepdims=True)
        expo = jnp.exp(scores - top)
        total = jnp.sum(expo, axis=1, keepdims=True)
        mixed = jnp.dot(expo.astype(jnp.bfloat16), values, preferred_element_type=jnp.float32)
        attn[:, span] = (mixed / total).astype(jnp.bfloat16)

    def token_copy(name, chunk, slot, peer):
        n, m = number(("a", name, chunk)), number(("a", slot, chunk))
        start, size = CHUNKS[chunk]
        span = pl.ds(start * HD, size * HD)
        return pltpu.make_async_remote_copy(
            src_ref=attn.at[:, span], dst_ref=toks.at[slot, :, span], send_sem=send_sems.at[n],
            recv_sem=recv_sems.at[m], device_id=peer, device_id_type=MESH,
        )

    def attention(chunk, bias):
        for way, slot in ((0, 3), (1, 5)):
            receive(("g", chunk, way), heads_of(slot, chunk))
        start, size = CHUNKS[chunk]
        for h in range(start, start + size):
            attention_head(h, bias)

        @pl.when(own)
        def _():
            token_copy("mate", chunk, 0, mate_core).start()
            span = slice(start * HD, (start + size) * HD)
            toks[0, :, span] = attn[:, span]

        @pl.when(jnp.logical_not(own))
        def _():
            token_copy("mate", chunk, 1, mate_core).start()
            token_copy("sib", chunk, 1, sibling).start()

    def tokens_in(chunk):
        @pl.when(jnp.logical_not(own))
        def _():
            token_copy(0, chunk, 0, sibling).wait_recv()

        token_copy(1, chunk, 1, sibling).wait_recv()

    def tokens_end(chunk):
        token_copy("mate", chunk, 1, mate_core).wait_send()

        @pl.when(jnp.logical_not(own))
        def _():
            token_copy("sib", chunk, 1, sibling).wait_send()

    def span_of(half):
        return (0, wcols) if half is None else HALVES[half]

    def project(piece, half=None):
        start, size = span_of(half)
        span = pl.ds(start, size)
        weights = wall[piece, :, span].reshape(NZ * size, heads * HD)
        tokens = toks[...].reshape(2 * TILE, heads * HD)
        partial = lax.dot_general(
            weights, tokens, (((1,), (1,)), ((), ())), preferred_element_type=jnp.float32
        )
        give[piece, :, span] = partial[:, TILE:].astype(jnp.bfloat16).reshape(NZ, size, TILE)
        send(("c", piece, half), give.at[piece, :, span], take.at[piece, :, span], sibling)
        keep[piece, :, span] = partial[:, :TILE].reshape(NZ, size, TILE)

    def scatter(piece, half=None):
        start, size = span_of(half)
        span = pl.ds(start, size)
        receive(("c", piece, half), take.at[piece, :, span])
        total = keep[piece, :, span] + take[piece, :, span].astype(jnp.float32)
        sbuf[piece, :, span] = total.astype(jnp.bfloat16)
        for r in ORDER:
            dst = rbuf.at[piece, f, span]
            to = fsdp_peer[r]
            send(("f", piece, half, r), sbuf.at[piece, to[0], span], dst, to)
        rbuf[piece, f, span] = sbuf[piece, f, span]

    def finish(piece, half=None):
        start, size = span_of(half)
        span = pl.ds(start, size)
        for r in ORDER:
            receive(("f", piece, half, r), rbuf.at[piece, wrap(f - r, groups), span])
        for part_half in range(2) if half is None else (half,):
            start, size = HALVES[part_half]
            span = pl.ds(start, size)
            from_yh = wrap(yh + OFFSETS[piece][part_half], NYH)
            for column_core, sources in ((0, (0, 3, 4, 7)), (1, (1, 2, 5, 6))):
                first = pl.multiple_of(from_yh * (2 * wcols) + column_core * wcols + start, 16)
                summed = jnp.zeros((size, TILE), jnp.float32)
                for source in sources:
                    summed = summed + rbuf[piece, source, span].astype(jnp.float32)
                gate = gcol[pl.ds(first, size), :]
                obuf[pl.ds(first, size), :] = (gate * summed).astype(obuf.dtype)
                out = pltpu.make_async_copy(
                    obuf.at[pl.ds(first, size)], out_ref.at[pl.ds(first, size)],
                    out_sems.at[(piece * 2 + part_half) * 2 + column_core],
                )
                out.start()
                written.append(out)

    swap()
    weights_out(1)
    ring_step(0, 1)
    weights_out(2)
    sibling_out()
    gate_column()
    bias = key_bias()
    receive(("s",), kv.at[1])
    ring_step(0, 2)
    halo(0)
    weights_in(1)
    weights_on()
    ring_step(1, 1)
    ring_step(0, 3)
    halo(1)
    ring_step(1, 2)
    ring_step(0, 4)
    weights_in(2)
    ring_step(2, 1)
    ring_step(1, 3)
    ring_step(2, 2)
    ring_step(1, 4)
    forward(0)
    weights_in(3)
    ring_step(3, 1)
    attention(0, bias)
    ring_step(2, 3)
    forward(1)
    ring_step(3, 2)
    attention(1, bias)
    ring_step(2, 4)
    ring_step(3, 3)
    ring_last(0)
    tokens_in(0)
    tokens_in(1)
    project(0)
    ring_last(1)
    project(1)
    scatter(0)
    ring_step(3, 4)
    scatter(1)
    ring_last(2)
    project(2)
    scatter(2)
    ring_last(3, (0,))
    project(3, 0)
    ring_last(3, (1,))
    project(3, 1)
    finish(0)
    scatter(3, 0)
    scatter(3, 1)
    finish(1)
    finish(2)
    finish(3, 0)
    finish(3, 1)
    tokens_end(0)
    tokens_end(1)
    for copy in started:
        copy.wait_send()
    for copy in written:
        copy.wait()


def on_device(q_heads, k_heads, v_heads, out_weight, out_gate, tile_map, key_tiles, key_count):
    tokens, width = q_heads.shape
    wcols = out_weight.shape[1]
    features = out_gate.shape[0]
    bf16 = jnp.bfloat16
    return pl.pallas_call(
        kernel,
        out_shape=jax.ShapeDtypeStruct((features, tokens), bf16),
        in_specs=[pl.BlockSpec(memory_space=pl.ANY)] * 8,
        out_specs=pl.BlockSpec(memory_space=pl.ANY),
        scratch_shapes=[
            pltpu.VMEM((TILE, width), bf16),
            pltpu.VMEM((6, 2, TILE, width), bf16),
            pltpu.VMEM((wcols, width), bf16),
            pltpu.VMEM((4, NZ, wcols, width), bf16),
            pltpu.VMEM((TILE, width), bf16),
            pltpu.VMEM((2, TILE, width), bf16),
            pltpu.VMEM((4, NZ, wcols, TILE), jnp.float32),
            pltpu.VMEM((4, NZ, wcols, TILE), bf16),
            pltpu.VMEM((4, NZ, wcols, TILE), bf16),
            pltpu.VMEM((4, NZ, wcols, TILE), bf16),
            pltpu.VMEM((4, NX * NYL, wcols, TILE), bf16),
            pltpu.VMEM((features,), jnp.float32),
            pltpu.VMEM((features, HD), jnp.float32),
            pltpu.SMEM(tile_map.shape, jnp.int32),
            pltpu.SMEM(key_tiles.shape[::-1], jnp.int32),
            pltpu.SMEM(key_count.shape, jnp.int32),
            pltpu.VMEM((features, tokens), bf16),
            pltpu.SemaphoreType.DMA((16,)),
            pltpu.SemaphoreType.DMA((8,)),
            pltpu.SemaphoreType.DMA((128,)),
            pltpu.SemaphoreType.DMA((128,)),
        ],
        compiler_params=pltpu.CompilerParams(
            collective_id=0, has_side_effects=True, vmem_limit_bytes=56 * 2**20
        ),
        cost_estimate=pl.CostEstimate(
            flops=1_100_000_000, bytes_accessed=2_000_000, transcendentals=500_000
        ),
        name="attend_project",
    )(q_heads, k_heads, v_heads, out_weight.T, out_gate, tile_map, key_tiles.T, key_count)


def solution(mesh):
    return jax.shard_map(
        on_device,
        mesh=mesh,
        in_specs=(
            P("seq", "fsdp"),
            P("seq", "fsdp"),
            P("seq", "fsdp"),
            P("fsdp", "seq"),
            P("fsdp"),
            P(),
            P(),
            P(),
        ),
        out_specs=P("fsdp", "seq"),
        check_vma=False,
    )
```

```python
import functools
import jax
import jax.numpy as jnp
from jax import lax
from jax.experimental import pallas as pl
from jax.experimental.pallas import tpu as pltpu
from jax.sharding import PartitionSpec as P

HD = 128
TILE = 128
KMAX = 4
NX, NYL, NZ, NYH = 4, 2, 8, 4
PLANES = NZ * NYH
NEG = -1e30
HALVES = ((0, 48), (48, 32))
MESH = pl.DeviceIdType.MESH


FEW = (1, 1)
ORDER = (2, 6, 1, 7, 3, 5, 4)
CHUNKS = ((0, 3), (3, 2))
OFFSETS = ((0, 0), (-1, 1), (1, -1), (2, 2))


def kernel(
    q_ref, k_ref, v_ref, w_ref, gate_ref, map_ref, list_ref, count_ref, out_ref,
    qbuf, kv, wtmp, wall, attn, toks, keep, give, take, sbuf, rbuf, gline, gcol,
    tile_map, key_list, key_count, obuf, out_sems, local_sems, send_sems, recv_sems,
):
    heads = q_ref.shape[1] // HD
    wcols = w_ref.shape[0]
    f = lax.axis_index("fsdp")
    s = lax.axis_index("seq")
    yl, x = f // NX, f % NX
    core, yh, z = s % 2, (s // 2) % NYH, s // 8
    plane = s // 2

    def seq_id(zz, yy, cc):
        return zz * 8 + yy * 2 + cc

    def wrap(a, n):
        return (a + n) % n

    sibling = (f, seq_id(z, yh, 1 - core))
    z_next = (f, seq_id(wrap(z + 1, NZ), yh, core))
    z_prev = (f, seq_id(wrap(z - 1, NZ), yh, core))
    y_next = (f, seq_id(z, wrap(yh + 1, NYH), core))
    y_prev = (f, seq_id(z, wrap(yh - 1, NYH), core))
    p_next = (f, wrap(plane + 1, PLANES) * 2 + core)
    p_prev = (f, wrap(plane - 1, PLANES) * 2 + core)
    kind = ((x + 1) // 2) % 2
    own = core == kind
    mate = yl * NX + x + 1 - 2 * (x % 2)
    swap_peer = (mate, seq_id(z, yh, 1 - core))
    mate_core = (mate, seq_id(z, yh, kind))
    groups = NX * NYL
    fsdp_peer = [(wrap(f + r, groups), s) for r in range(groups)]

    peers = [sibling, z_next, z_prev, y_next, y_prev, p_next, p_prev, swap_peer] + fsdp_peer[1:]
    local = [
        pltpu.make_async_copy(src, dst, local_sems.at[n])
        for n, (src, dst) in enumerate((
            (w_ref, wtmp), (k_ref, kv.at[0, 0]), (v_ref, kv.at[0, 1]), (q_ref, qbuf),
            (gate_ref, gline), (map_ref, tile_map), (list_ref, key_list), (count_ref, key_count),
        ))
    ]
    for copy in local:
        copy.start()
    barrier = pltpu.get_barrier_semaphore()
    for peer in peers:
        pl.semaphore_signal(barrier, inc=1, device_id=peer, device_id_type=MESH)

    def gate_column():
        local[4].wait()
        rows = lax.broadcasted_iota(jnp.int32, (HD, HD), 0)
        cols = lax.broadcasted_iota(jnp.int32, (HD, HD), 1)
        for i in range(gline.shape[0] // HD):
            line = jnp.broadcast_to(gline[i * HD:(i + 1) * HD].reshape(1, HD), (HD, HD))
            column = jnp.sum(jnp.where(rows == cols, line, 0.0), axis=1, keepdims=True)
            gcol[i * HD:(i + 1) * HD, :] = jnp.broadcast_to(column, (HD, HD))

    for copy in local[:4]:
        copy.wait()
    pl.semaphore_wait(barrier, len(peers))

    started = []
    written = []
    table = {}

    def number(key):
        return table.setdefault(key, len(table))

    def send(key, src, dst, peer):
        n = number(key)
        copy = pltpu.make_async_remote_copy(
            src_ref=src, dst_ref=dst, send_sem=send_sems.at[n], recv_sem=recv_sems.at[n],
            device_id=peer, device_id_type=MESH,
        )
        copy.start()
        started.append(copy)

    def receive(key, dst):
        n = number(key)
        pltpu.make_async_remote_copy(
            src_ref=dst, dst_ref=dst, send_sem=send_sems.at[n], recv_sem=recv_sems.at[n],
            device_id=sibling, device_id_type=MESH,
        ).wait_recv()

    def swap():
        n = number("swap")
        copy = pltpu.make_async_remote_copy(
            src_ref=wtmp, dst_ref=wall.at[0, z], send_sem=send_sems.at[n],
            recv_sem=recv_sems.at[n], device_id=swap_peer, device_id_type=MESH,
        )

        @pl.when(own)
        def _():
            wall[0, z] = wtmp[...]

        @pl.when(jnp.logical_not(own))
        def _():
            copy.start()
            copy.wait()

    def part(piece, zz, half):
        start, size = HALVES[half]
        return wall.at[piece, zz, pl.ds(start, size)]

    def ring_pieces(hop):
        return (wrap(z - hop, NZ), wrap(z + hop, NZ))

    def last_way(piece, half):
        inner = (piece + half) % 2
        low, high = (0, 1) if (piece, half) == FEW else (1, 0)
        return jnp.where(yh == 0, low, jnp.where(yh == NYH - 1, high, inner))

    def ring_step(piece, hop):
        for half in range(2):
            if hop > 1:
                for way, zz in enumerate(ring_pieces(hop - 1)):
                    receive(("z", piece, half, way, hop - 1), part(piece, zz, half))
                    if hop < 4:
                        ref = part(piece, zz, half)
                        send(("z", piece, half, way, hop), ref, ref, (z_next, z_prev)[way])
            else:
                for way in range(2):
                    ref = part(piece, z, half)
                    send(("z", piece, half, way, 1), ref, ref, (z_next, z_prev)[way])
            if hop == 4:
                turn = 2 * last_way(piece, half) - 1
                ref = part(piece, wrap(z + 3 * turn, NZ), half)
                peer = (f, seq_id(wrap(z - turn, NZ), yh, core))
                send(("z", piece, half, 4), ref, ref, peer)

    def ring_last(piece, halves=(0, 1)):
        for half in halves:
            receive(("z", piece, half, 4), part(piece, wrap(z + 4, NZ), half))

    def rows(piece, half):
        return part(piece, z, half)

    def weights_out(piece):
        for half in range(2):
            peer = y_next if (half == 0) == (piece == 1) else y_prev
            send(("y", piece, half), rows(0, half), rows(piece, half), peer)

    def weights_in(piece):
        for half in range(2):
            receive(("y", piece, half), rows(piece, half))

    def weights_on():
        for half, peer in ((0, y_next), (1, y_prev)):
            send(("y", 3, half), rows(1, half), rows(3, half), peer)

    def sibling_out():
        send(("s",), kv.at[0], kv.at[1], sibling)

    def heads_of(slot, chunk):
        start, size = CHUNKS[chunk]
        return kv.at[slot, :, :, pl.ds(start * HD, size * HD)]

    def halo(chunk):
        send(("h", chunk, 0), heads_of(0, chunk), heads_of(2, chunk), p_next)
        send(("h", chunk, 1), heads_of(0, chunk), heads_of(4, chunk), p_prev)

    def forward(chunk):
        for way, slot in ((0, 2), (1, 4)):
            receive(("h", chunk, way), heads_of(slot, chunk))
            send(("g", chunk, way), heads_of(slot, chunk), heads_of(slot + 1, chunk), sibling)

    def key_bias():
        for copy in local[5:]:
            copy.wait()
        tile = tile_map[s]
        used = key_count[tile]
        listed = [key_list[i, tile] for i in range(KMAX)]
        below, above = wrap(plane - 1, PLANES), wrap(plane + 1, PLANES)
        slots = (
            (s, None), (plane * 2 + 1 - core, None),
            (below * 2 + core, plane > 0), (below * 2 + 1 - core, plane > 0),
            (above * 2 + core, plane < PLANES - 1), (above * 2 + 1 - core, plane < PLANES - 1),
        )
        lane_tile = lax.broadcasted_iota(jnp.int32, (1, 6 * TILE), 1) // TILE
        bias = jnp.zeros((1, 6 * TILE), jnp.float32)
        for n, (slot, inside) in enumerate(slots):
            other = tile_map[slot]
            hit = jnp.int32(0)
            for i in range(KMAX):
                same = jnp.where(listed[i] == other, 1, 0) * jnp.where(used > i, 1, 0)
                hit = jnp.maximum(hit, same)
            if inside is not None:
                hit = hit * jnp.where(inside, 1, 0)
            value = jnp.where(hit == 1, 0.0, NEG).astype(jnp.float32)
            bias = jnp.where(lane_tile == n, value, bias)
        return bias

    def attention_head(h, bias):
        span = slice(h * HD, (h + 1) * HD)
        keys = kv[:, 0, :, span].reshape(6 * TILE, HD)
        values = kv[:, 1, :, span].reshape(6 * TILE, HD)
        scores = lax.dot_general(
            qbuf[:, span], keys, (((1,), (1,)), ((), ())), preferred_element_type=jnp.float32
        )
        scores = scores * (1.0 / float(HD) ** 0.5) + bias
        top = jnp.max(scores, axis=1, keepdims=True)
        expo = jnp.exp(scores - top)
        total = jnp.sum(expo, axis=1, keepdims=True)
        mixed = jnp.dot(expo.astype(jnp.bfloat16), values, preferred_element_type=jnp.float32)
        attn[:, span] = (mixed / total).astype(jnp.bfloat16)

    def token_copy(name, chunk, slot, peer):
        n, m = number(("a", name, chunk)), number(("a", slot, chunk))
        start, size = CHUNKS[chunk]
        span = pl.ds(start * HD, size * HD)
        return pltpu.make_async_remote_copy(
            src_ref=attn.at[:, span], dst_ref=toks.at[slot, :, span], send_sem=send_sems.at[n],
            recv_sem=recv_sems.at[m], device_id=peer, device_id_type=MESH,
        )

    def attention(chunk, bias):
        for way, slot in ((0, 3), (1, 5)):
            receive(("g", chunk, way), heads_of(slot, chunk))
        start, size = CHUNKS[chunk]
        for h in range(start, start + size):
            attention_head(h, bias)

        @pl.when(own)
        def _():
            token_copy("mate", chunk, 0, mate_core).start()
            span = slice(start * HD, (start + size) * HD)
            toks[0, :, span] = attn[:, span]

        @pl.when(jnp.logical_not(own))
        def _():
            token_copy("mate", chunk, 1, mate_core).start()
            token_copy("sib", chunk, 1, sibling).start()

    def tokens_in(chunk):
        @pl.when(jnp.logical_not(own))
        def _():
            token_copy(0, chunk, 0, sibling).wait_recv()

        token_copy(1, chunk, 1, sibling).wait_recv()

    def tokens_end(chunk):
        token_copy("mate", chunk, 1, mate_core).wait_send()

        @pl.when(jnp.logical_not(own))
        def _():
            token_copy("sib", chunk, 1, sibling).wait_send()

    def span_of(half):
        return (0, wcols) if half is None else HALVES[half]

    def project(piece, half=None):
        start, size = span_of(half)
        span = pl.ds(start, size)
        weights = wall[piece, :, span].reshape(NZ * size, heads * HD)
        tokens = toks[...].reshape(2 * TILE, heads * HD)
        partial = lax.dot_general(
            weights, tokens, (((1,), (1,)), ((), ())), preferred_element_type=jnp.float32
        )
        give[piece, :, span] = partial[:, TILE:].astype(jnp.bfloat16).reshape(NZ, size, TILE)
        send(("c", piece, half), give.at[piece, :, span], take.at[piece, :, span], sibling)
        keep[piece, :, span] = partial[:, :TILE].reshape(NZ, size, TILE)

    def scatter(piece, half=None):
        start, size = span_of(half)
        span = pl.ds(start, size)
        receive(("c", piece, half), take.at[piece, :, span])
        total = keep[piece, :, span] + take[piece, :, span].astype(jnp.float32)
        sbuf[piece, :, span] = total.astype(jnp.bfloat16)
        for r in ORDER:
            dst = rbuf.at[piece, f, span]
            to = fsdp_peer[r]
            send(("f", piece, half, r), sbuf.at[piece, to[0], span], dst, to)
        rbuf[piece, f, span] = sbuf[piece, f, span]

    def finish(piece, half=None):
        start, size = span_of(half)
        span = pl.ds(start, size)
        for r in ORDER:
            receive(("f", piece, half, r), rbuf.at[piece, wrap(f - r, groups), span])
        for part_half in range(2) if half is None else (half,):
            start, size = HALVES[part_half]
            span = pl.ds(start, size)
            from_yh = wrap(yh + OFFSETS[piece][part_half], NYH)
            for column_core, sources in ((0, (0, 3, 4, 7)), (1, (1, 2, 5, 6))):
                first = pl.multiple_of(from_yh * (2 * wcols) + column_core * wcols + start, 16)
                summed = jnp.zeros((size, TILE), jnp.float32)
                for source in sources:
                    summed = summed + rbuf[piece, source, span].astype(jnp.float32)
                gate = gcol[pl.ds(first, size), :]
                obuf[pl.ds(first, size), :] = (gate * summed).astype(obuf.dtype)
                out = pltpu.make_async_copy(
                    obuf.at[pl.ds(first, size)], out_ref.at[pl.ds(first, size)],
                    out_sems.at[(piece * 2 + part_half) * 2 + column_core],
                )
                out.start()
                written.append(out)

    swap()
    weights_out(1)
    ring_step(0, 1)
    weights_out(2)
    sibling_out()
    gate_column()
    bias = key_bias()
    receive(("s",), kv.at[1])
    ring_step(0, 2)
    halo(0)
    weights_in(1)
    weights_on()
    ring_step(1, 1)
    ring_step(0, 3)
    halo(1)
    ring_step(1, 2)
    ring_step(0, 4)
    weights_in(2)
    ring_step(2, 1)
    ring_step(1, 3)
    ring_step(2, 2)
    ring_step(1, 4)
    forward(0)
    weights_in(3)
    ring_step(3, 1)
    attention(0, bias)
    ring_step(2, 3)
    forward(1)
    ring_step(3, 2)
    attention(1, bias)
    ring_step(2, 4)
    ring_step(3, 3)
    ring_last(0)
    tokens_in(0)
    tokens_in(1)
    project(0)
    ring_last(1)
    project(1)
    scatter(0)
    ring_step(3, 4)
    scatter(1)
    ring_last(2)
    project(2)
    scatter(2)
    ring_last(3)
    project(3)
    finish(0)
    scatter(3)
    finish(1)
    finish(2)
    finish(3)
    tokens_end(0)
    tokens_end(1)
    for copy in started:
        copy.wait_send()
    for copy in written:
        copy.wait()


def on_device(q_heads, k_heads, v_heads, out_weight, out_gate, tile_map, key_tiles, key_count):
    tokens, width = q_heads.shape
    wcols = out_weight.shape[1]
    features = out_gate.shape[0]
    bf16 = jnp.bfloat16
    return pl.pallas_call(
        kernel,
        out_shape=jax.ShapeDtypeStruct((features, tokens), bf16),
        in_specs=[pl.BlockSpec(memory_space=pl.ANY)] * 8,
        out_specs=pl.BlockSpec(memory_space=pl.ANY),
        scratch_shapes=[
            pltpu.VMEM((TILE, width), bf16),
            pltpu.VMEM((6, 2, TILE, width), bf16),
            pltpu.VMEM((wcols, width), bf16),
            pltpu.VMEM((4, NZ, wcols, width), bf16),
            pltpu.VMEM((TILE, width), bf16),
            pltpu.VMEM((2, TILE, width), bf16),
            pltpu.VMEM((4, NZ, wcols, TILE), jnp.float32),
            pltpu.VMEM((4, NZ, wcols, TILE), bf16),
            pltpu.VMEM((4, NZ, wcols, TILE), bf16),
            pltpu.VMEM((4, NZ, wcols, TILE), bf16),
            pltpu.VMEM((4, NX * NYL, wcols, TILE), bf16),
            pltpu.VMEM((features,), jnp.float32),
            pltpu.VMEM((features, HD), jnp.float32),
            pltpu.SMEM(tile_map.shape, jnp.int32),
            pltpu.SMEM(key_tiles.shape[::-1], jnp.int32),
            pltpu.SMEM(key_count.shape, jnp.int32),
            pltpu.VMEM((features, tokens), bf16),
            pltpu.SemaphoreType.DMA((16,)),
            pltpu.SemaphoreType.DMA((8,)),
            pltpu.SemaphoreType.DMA((128,)),
            pltpu.SemaphoreType.DMA((128,)),
        ],
        compiler_params=pltpu.CompilerParams(
            collective_id=0, has_side_effects=True, vmem_limit_bytes=56 * 2**20
        ),
        cost_estimate=pl.CostEstimate(
            flops=1_100_000_000, bytes_accessed=2_000_000, transcendentals=500_000
        ),
        name="attend_project",
    )(q_heads, k_heads, v_heads, out_weight.T, out_gate, tile_map, key_tiles.T, key_count)


def solution(mesh):
    return jax.shard_map(
        on_device,
        mesh=mesh,
        in_specs=(
            P("seq", "fsdp"),
            P("seq", "fsdp"),
            P("seq", "fsdp"),
            P("fsdp", "seq"),
            P("fsdp"),
            P(),
            P(),
            P(),
        ),
        out_specs=P("fsdp", "seq"),
        check_vma=False,
    )
```
